512 devices in a mesh: row: 16 (over x_hi, y, core), col: 32 (over x_lo, z).
Axes of the slice: x: 4 (x_hi: 2, x_lo: 2; x = x_hi * 2 + x_lo), y: 4, z: 16, core: 2. Of those that a mesh axis runs over, the one named last changes fastest.
Arguments:
- activations: bfloat16 [1024, 14848], P('col', 'row'), may hold values from -0.29882812 to 0.29882812
- out_grad: bfloat16 [1024, 29696], P('row', 'col'), may hold values from -4.1875 to 4.1875
- weight: bfloat16 [14848, 29696], P('row', 'col'), may hold values from -0.046875 to 0.046875
Outputs:
- d_input: bfloat16 [1024, 14848], P('col', 'row')
- d_weight: bfloat16 [14848, 29696], P('row', 'col')
The draws below stay inside these ranges and needn't reach their ends.
All inputs are finite; a program needn't handle non-finite values.
Results may differ from the reference program's by a relative error of at most 0.001.
Values may be sent and summed in bfloat16 or wider, within the bound.
A program may use at most 64 MiB of HBM per device.

```python
import jax
import jax.numpy as jnp

D = 14848
FW = 29696
TOKENS = 1024


def with_spikes(entries, rng, source, target, parts, factor):
    owner, partner = [(jnp.arange(entries.shape[position]) // (entries.shape[position] // parts)).reshape([-1 if axis == position else 1 for axis in range(entries.ndim)]) for position in (source, target)]
    chosen = jax.random.permutation(rng, parts)[partner]
    strong = (owner == chosen) | (owner == (partner + parts // 2) % parts)
    return jnp.where(strong, factor * entries, entries)


def level_of(own_key, shape, shards, least, top_value):
    level = 1.0
    for dim, parts in shards:
        steps = jax.random.uniform(jax.random.fold_in(jax.random.fold_in(own_key, 6), dim), (parts,), jnp.float32, least / len(shards), top_value / len(shards))
        level = level * jnp.repeat(jnp.exp(steps), shape[dim] // parts).reshape((-1,) + (1,) * (len(shape) - 1 - dim))
    return level


def centred(own_key, dims, width, reach, shards=(), dtype=jnp.bfloat16):
    drawn = width * jax.random.normal(own_key, dims, jnp.float32)
    if shards:
        drawn = drawn * level_of(own_key, dims, shards, -0.22, 0.18)
    return jnp.clip(drawn, -reach, reach).astype(dtype)


def heavy_noise(stream_key, shape, deviation, most, shards, heavy, held_as=jnp.bfloat16):
    result = deviation * jax.random.normal(stream_key, shape, jnp.float32)
    if shards:
        result = result * level_of(stream_key, shape, shards, -0.22, 0.18)
    return jnp.clip(with_spikes(result, jax.random.fold_in(stream_key, 3), *heavy), -most, most).astype(held_as)


def setup_inputs(seed: int = 0) -> dict:
    seeds = jax.random.split(jax.random.key(seed), 4)
    activations = centred(seeds[0], (TOKENS, D), 0.05, 0.29882812, ((0, 32), (1, 16)))
    out_grad = heavy_noise(seeds[1], (TOKENS, FW), 0.7, 4.1875, ((0, 16), (1, 32)), (1, 0, 32, 2.75))
    weight = centred(seeds[2], (D, FW), D ** -0.5, 0.046875, ((0, 16), (1, 32)))
    return {"activations": activations, "out_grad": out_grad, "weight": weight}


def reference(activations, out_grad, weight):
    d_input = jnp.dot(out_grad, weight.T, preferred_element_type=jnp.float32).astype(jnp.bfloat16)
    d_weight = jnp.dot(activations.T, out_grad, preferred_element_type=jnp.float32).astype(jnp.bfloat16)
    return d_input, d_weight
```

```python
import functools

import jax
import jax.numpy as jnp
from jax import lax
from jax.experimental import pallas as pl
from jax.experimental.pallas import tpu as pltpu
from jax.sharding import PartitionSpec as P

MESH = pl.DeviceIdType.MESH
F32 = jnp.float32
BF16 = jnp.bfloat16
Y, Z = 4, 16
HALF = Z // 2
T = 32
S = 16


def kernel(act_hbm, og_hbm, w_hbm, din_ref, dw_ref,
           act, og, w, part, xpart, ring, last,
           local_sem, r_send, r_recv, d_send, d_recv, a_send, a_recv, c_send, c_recv,
           x_send, x_recv, s_send, s_recv, l_send, l_recv):
    row, col = lax.axis_index("row"), lax.axis_index("col")
    xh, y, core = row // 8, (row // 2) % Y, row % 2
    xl, z = col // Z, col % Z

    def device(dx=0, dy=0, dcore=0, dl=0, dz=0):
        r = ((xh + dx) % 2) * 8 + ((y + dy) % Y) * 2 + (core + dcore) % 2
        c = ((xl + dl) % 2) * Z + (z + dz) % Z
        return (r, c)

    def owner_at(line, zz):
        return pl.multiple_of((zz // 4) * 256 + line * 128 + (zz % 4) * T, T)

    def source_at(hi, yy, cc):
        return pl.multiple_of(yy * 256 + hi * 128 + cc * 64, 64)

    def remote(src, dst, send, recv, **where):
        return pltpu.make_async_remote_copy(
            src_ref=src, dst_ref=dst, send_sem=send, recv_sem=recv,
            device_id=device(**where), device_id_type=MESH)

    own_og = og.at[pl.ds(source_at(xh, y, core), 64)]
    own_act = act.at[pl.ds(owner_at(xl, z), T)]
    get_og = pltpu.make_async_copy(og_hbm, own_og, local_sem.at[0])
    get_act = pltpu.make_async_copy(act_hbm, own_act, local_sem.at[1])
    get_w = pltpu.make_async_copy(w_hbm, w, local_sem.at[2])
    get_og.start()
    get_act.start()
    get_w.start()

    peers = [(dx, dy) for dy in (1, 3, 0, 2) for dx in (0, 1) if (dx, dy) != (0, 0)]
    barrier = pltpu.get_barrier_semaphore()
    near = [dict(dx=dx, dy=dy) for dx, dy in peers]
    near += [dict(dcore=1), dict(dl=1), dict(dz=1), dict(dz=Z - 1)]
    for where in near:
        pl.semaphore_signal(barrier, inc=1, device_id=device(**where), device_id_type=MESH)
    pl.semaphore_wait(barrier, len(near))

    waits = []

    def go(copy):
        copy.start()
        waits.append(copy)

    get_og.wait()
    for dx, dy in [(1, 0), (0, 1), (0, 3), (0, 2), (1, 1), (1, 3), (1, 2)]:
        go(remote(own_og, own_og, r_send.at[dx, dy], r_recv.at[dx, (Y - dy) % Y], dx=dx, dy=dy))
    go(remote(own_og, own_og, d_send.at[0, 0], d_recv.at[0, 0], dcore=1))

    get_act.wait()
    go(remote(own_act, own_act, a_send, a_recv, dl=1))

    def act_hop(line, way, step):
        zz = (z - (step - 1)) % Z if way == 0 else (z + (step - 1)) % Z
        block = act.at[pl.ds(owner_at((xl + line) % 2, zz), T)]
        return remote(block, block, c_send.at[line, way, step], c_recv.at[line, way, step],
                      dz=1 if way == 0 else Z - 1)

    hops = [HALF, HALF - 1]

    def act_step(line, step):
        for way in (0, 1):
            if step >= 2 and step - 1 <= hops[way]:
                act_hop(line, way, step - 1).wait_recv()
            if step <= hops[way]:
                go(act_hop(line, way, step))

    act_step(0, 1)
    remote(own_act, own_act, a_send, a_recv, dl=1).wait_recv()
    act_step(1, 1)

    def share(dx, dy):
        block = og.at[pl.ds(source_at((xh + dx) % 2, (y + dy) % Y, core), 64)]
        if (dx, dy) != (0, 0):
            remote(block, block, r_send.at[dx, dy], r_recv.at[dx, dy], dx=dx, dy=dy).wait_recv()
            go(remote(block, block, d_send.at[dx, dy], d_recv.at[dx, dy], dcore=1))

    def shared(dx, dy):
        block = og.at[pl.ds(source_at((xh + dx) % 2, (y + dy) % Y, (core + 1) % 2), 64)]
        remote(block, block, d_send.at[dx, dy], d_recv.at[dx, dy], dcore=1).wait_recv()

    def product(dy):
        rows = pl.ds(pl.multiple_of(((y + dy) % Y) * 256, 256), 256)
        part[rows, :] = lax.dot_general(
            og[rows, :], w[...], (((1,), (1,)), ((), ())), preferred_element_type=F32)

    def cross(dz):
        zz = (z + dz) % Z
        rows = part.at[pl.ds(owner_at((xl + 1) % 2, zz), S)]
        return remote(rows, xpart.at[zz], x_send.at[zz], x_recv.at[zz], dl=1)

    def cross_group(dy):
        for i in range(4):
            zz = ((y + dy) % Y) * 4 + i
            rows = part.at[pl.ds(owner_at((xl + 1) % 2, zz), S)]
            go(remote(rows, xpart.at[zz], x_send.at[zz], x_recv.at[zz], dl=1))

    share(1, 0)
    share(0, 1)
    share(0, 3)
    get_w.wait()
    shared(0, 0)
    shared(1, 0)
    product(0)
    cross_group(0)
    act_step(0, 2)
    act_step(1, 2)
    share(1, 1)
    share(1, 3)
    share(0, 2)
    share(1, 2)
    for dy in (1, 3, 2):
        for dx in (0, 1):
            shared(dx, dy)
        product(dy)
        cross_group(dy)
    act_step(0, 3)
    act_step(1, 3)

    def piece(p, zz):
        line = (xl + (1 if p == 1 else 0)) % 2
        return part.at[pl.ds(owner_at(line, zz) + (0 if p == 2 else S), S)]

    def sum_hop(way, k, p):
        d = HALF - k
        zz = (z + d) % Z if way == 0 else (z + Z - d) % Z
        src = piece(p, zz) if k == first[way] else ring.at[way, k - 1, p]
        return remote(src, ring.at[way, k, p], s_send.at[way, k, p], s_recv.at[way, k, p],
                      dz=1 if way == 0 else Z - 1)

    first = [0, 1]

    def sum_step(k):
        for p in range(3):
            for way in (0, 1):
                if k < first[way]:
                    continue
                d = HALF - k
                zz = (z + d) % Z if way == 0 else (z + Z - d) % Z
                mine = piece(p, zz)
                if p == 2:
                    cross(d if way == 0 else Z - d).wait_recv()
                    mine[...] += xpart[zz]
                if k > first[way]:
                    sum_hop(way, k - 1, p).wait_recv()
                    ring[way, k - 1, p] = ring[way, k - 1, p] + mine[...]
                go(sum_hop(way, k, p))

    def weight_grad(start, width):
        cols = pl.ds(start, width)
        dw_ref[:, cols] = lax.dot_general(
            act[...], og[:, cols], (((0,), (0,)), ((), ())),
            preferred_element_type=F32).astype(BF16)

    for k in range(HALF):
        sum_step(k)
        if k + 4 <= HALF + 1:
            act_step(0, k + 4)
            act_step(1, k + 4)
        if k == 6:
            weight_grad(0, 256)
            weight_grad(256, 256)
        if k == 7:
            weight_grad(512, 256)
            weight_grad(768, 160)

    def total(p):
        mine = piece(p, z)
        acc = mine[...]
        if p == 2:
            cross(0).wait_recv()
            acc += xpart[z]
        for way in (0, 1):
            sum_hop(way, HALF - 1, p).wait_recv()
            acc += ring[way, HALF - 1, p]
        return acc

    other = total(1)
    mine = piece(1, z)
    mine[...] = other
    swap = remote(mine, last, l_send, l_recv, dl=1)
    go(swap)
    acc = total(0)
    din_ref[:S, :] = total(2).astype(BF16)
    swap.wait_recv()
    din_ref[S:, :] = (acc + last[...]).astype(BF16)
    for copy in waits:
        copy.wait_send()


def on_device(activations, out_grad, weight):
    model, hidden = weight.shape
    dma = pltpu.SemaphoreType.DMA
    return pl.pallas_call(
        kernel,
        out_shape=(jax.ShapeDtypeStruct(activations.shape, BF16), jax.ShapeDtypeStruct(weight.shape, BF16)),
        in_specs=[pl.BlockSpec(memory_space=pl.ANY)] * 3,
        out_specs=(pl.BlockSpec(memory_space=pltpu.VMEM), pl.BlockSpec(memory_space=pltpu.VMEM)),
        scratch_shapes=[
            pltpu.VMEM((2 * Z * T, model), BF16),
            pltpu.VMEM((2 * Z * T, hidden), BF16),
            pltpu.VMEM((model, hidden), BF16),
            pltpu.VMEM((2 * Z * T, model), F32),
            pltpu.VMEM((Z, S, model), F32),
            pltpu.VMEM((2, HALF, 3, S, model), F32),
            pltpu.VMEM((S, model), F32),
            dma((3,)),
            dma((2, Y)), dma((2, Y)),
            dma((2, Y)), dma((2, Y)),
            dma(()), dma(()),
            dma((2, 2, HALF + 1)), dma((2, 2, HALF + 1)),
            dma((Z,)), dma((Z,)),
            dma((2, HALF, 3)), dma((2, HALF, 3)),
            dma(()), dma(()),
        ],
        compiler_params=pltpu.CompilerParams(
            collective_id=0, has_side_effects=True, vmem_limit_bytes=48 << 20),
        name="backward",
    )(activations, out_grad, weight)


def solution(mesh):
    return jax.shard_map(
        on_device,
        mesh=mesh,
        in_specs=(P("col", "row"), P("row", "col"), P("row", "col")),
        out_specs=(P("col", "row"), P("row", "col")),
        check_vma=False,
    )
```

```python
import jax
import jax.numpy as jnp
from jax import lax
from jax.experimental import pallas as pl
from jax.experimental.pallas import tpu as pltpu
from jax.sharding import PartitionSpec as P

MESH = pl.DeviceIdType.MESH
F32 = jnp.float32
BF16 = jnp.bfloat16
FLAGS = set()
Y, Z = 4, 16
HALF = Z // 2
WIDE = 7
MAIN = WIDE * 128
OG = 4 * WIDE + 1
ACT = 2 * WIDE + 1
SUM = 4 * WIDE + 1
OG_CUT = (0, 2 * WIDE, OG)
ACT_X = 8
SUM_X = 18
LAST = SUM - SUM_X
PIECES = (
    (0, SUM_X, LAST, 1),
    (LAST, SUM_X, LAST, 0),
    (2 * LAST, 0, SUM_X // 2, 0),
    (2 * LAST + SUM_X // 2, SUM_X // 2, SUM_X - SUM_X // 2, 0),
)
SLOT = 2 * LAST + SUM_X
FIRST = ((0, 1), (0, 1), (1, 0), (1, 0))


def kernel(act_hbm, og_hbm, w_hbm, din_ref, dw_hbm,
           act, og, w, wtail, act_pk, og_pk, part, xpart, ring, last, dw,
           local_sem, out_sem, r_send, r_recv, d_send, d_recv, a_send, a_recv, b_send, b_recv,
           c_send, c_recv, x_send, x_recv, s_send, s_recv, l_send, l_recv):
    row, col = lax.axis_index("row"), lax.axis_index("col")
    xh, y, core = row // 8, (row // 2) % Y, row % 2
    xl, z = col // Z, col % Z

    def device(dx=0, dy=0, dcore=0, dl=0, dz=0):
        r = ((xh + dx) % 2) * 8 + ((y + dy) % Y) * 2 + (core + dcore) % 2
        c = ((xl + dl) % 2) * Z + (z + dz) % Z
        return (r, c)

    def owner_at(line, zz):
        return (zz // 4) * 8 + line * 4 + zz % 4

    def source_at(hi, yy, cc):
        return yy * 4 + hi * 2 + cc

    def remote(src, dst, send, recv, **where):
        return pltpu.make_async_remote_copy(
            src_ref=src, dst_ref=dst, send_sem=send, recv_sem=recv,
            device_id=device(**where), device_id_type=MESH)

    waits = []

    def go(copy):
        copy.start()
        waits.append(copy)

    mine_og, mine_act = source_at(xh, y, core), owner_at(xl, z)
    get_og = pltpu.make_async_copy(
        og_hbm, og.at[pl.ds(pl.multiple_of(mine_og * 64, 64), 64)], local_sem.at[0])
    get_act = pltpu.make_async_copy(
        act_hbm, act.at[pl.ds(pl.multiple_of(mine_act * 32, 32), 32)], local_sem.at[1])
    get_w = pltpu.make_async_copy(w_hbm, w, local_sem.at[2])
    get_og.start()
    get_act.start()
    get_w.start()

    barrier = pltpu.get_barrier_semaphore()
    near = [dict(dx=1), dict(dy=1), dict(dy=3), dict(dy=2),
            dict(dcore=1), dict(dl=1), dict(dz=1), dict(dz=Z - 1)]
    for where in near:
        pl.semaphore_signal(barrier, inc=1, device_id=device(**where), device_id_type=MESH)

    def pack(rows_ref, base, groups, pk, place):
        tails = []
        for i in range(groups):
            rows = pl.ds(pl.multiple_of(base + 16 * i, 16), 16)
            for j in range(WIDE):
                pk[place, i * WIDE + j] = rows_ref[rows, j * 128:(j + 1) * 128]
            tails.append(rows_ref[rows, MAIN:])
        pk[place, groups * WIDE, :, :32 * groups] = jnp.concatenate(tails, axis=1)

    def unpack(pk, place, groups, rows_ref, base):
        tails = pk[place, groups * WIDE]
        for i in range(groups):
            rows = pl.ds(pl.multiple_of(base + 16 * i, 16), 16)
            for j in range(WIDE):
                rows_ref[rows, j * 128:(j + 1) * 128] = pk[place, i * WIDE + j]
            rows_ref[rows, MAIN:] = tails[:, 32 * i:32 * (i + 1)]

    get_og.wait()
    pack(og, mine_og * 64, 4, og_pk, mine_og)
    get_act.wait()
    pack(act, mine_act * 32, 2, act_pk, mine_act)
    pl.semaphore_wait(barrier, len(near))

    def og_piece(dx, dy, dcore, p):
        place = source_at((xh + dx) % 2, (y + dy) % Y, (core + dcore) % 2)
        return og_pk.at[place, pl.ds(OG_CUT[p], OG_CUT[p + 1] - OG_CUT[p])]

    def to_x(p):
        ref = og_piece(0, 0, 0, p)
        return remote(ref, ref, r_send.at[1, 0, p], r_recv.at[1, 0, p], dx=1)

    def to_y(dx, dy, p):
        ref = og_piece(dx, 0, 0, p)
        return remote(ref, ref, r_send.at[dx, dy, p], r_recv.at[dx, (Y - dy) % Y, p], dy=dy)

    def to_core(dx, dy, p):
        ref = og_piece(dx, dy, 0, p)
        return remote(ref, ref, d_send.at[dx, dy, p], d_recv.at[dx, dy, p], dcore=1)

    def arrived(dx, dy, p):
        ref = og_piece(dx, dy, 0, p)
        remote(ref, ref, r_send.at[dx, dy, p], r_recv.at[dx, dy, p], dx=1).wait_recv()

    def shared(dx, dy, p):
        ref = og_piece(dx, dy, 1, p)
        remote(ref, ref, d_send.at[dx, dy, p], d_recv.at[dx, dy, p], dcore=1).wait_recv()

    for p in (0, 1):
        go(to_x(p))
    for p in (0, 1):
        for dy in (1, 3):
            go(to_y(0, dy, p))
    for p in (0, 1):
        go(to_y(0, 2, p))

    def act_x(first_tiles, zz):
        cut = pl.ds(0, ACT_X) if first_tiles else pl.ds(ACT_X, ACT - ACT_X)
        ref = act_pk.at[owner_at(xl, zz), cut]
        if first_tiles:
            return remote(ref, ref, a_send, a_recv, dl=1)
        return remote(ref, ref, b_send.at[zz], b_recv.at[zz], dl=1)

    def act_hop(line, way, step):
        zz = (z - (step - 1)) % Z if way == 0 else (z + (step - 1)) % Z
        ref = act_pk.at[owner_at((xl + line) % 2, zz), pl.ds(0, ACT if line == 0 else ACT_X)]
        return remote(ref, ref, c_send.at[line, way, step], c_recv.at[line, way, step],
                      dz=1 if way == 0 else Z - 1)

    hops = (HALF, HALF - 1)

    def act_step(line, step):
        if "noC" in FLAGS:
            return
        for way in (0, 1):
            if step >= 2 and step - 1 <= hops[way]:
                act_hop(line, way, step - 1).wait_recv()
            if step <= hops[way]:
                go(act_hop(line, way, step))
            if line == 0 and step >= 2 and step - 1 <= hops[way]:
                go(act_x(False, (z - (step - 1)) % Z if way == 0 else (z + (step - 1)) % Z))

    go(act_x(True, z))
    act_step(0, 1)
    go(act_x(False, z))
    for p in (0, 1):
        go(to_core(0, 0, p))

    get_w.wait()
    for i in range(4):
        wtail[32 * i:32 * (i + 1), :] = w[MAIN:, :]

    for p in (0, 1):
        arrived(1, 0, p)
        for dy in (1, 3, 2):
            go(to_y(1, dy, p))
        go(to_core(1, 0, p))
    act_x(True, z).wait_recv()
    act_step(1, 1)
    for p in (0, 1):
        for dy in (1, 3):
            arrived(0, dy, p)
            go(to_core(0, dy, p))

    lane = lax.broadcasted_iota(jnp.int32, (8, 128), 1) // 32

    def product(dy):
        group = (y + dy) % Y
        if "noP" in FLAGS:
            return
        for i in range(4):
            unpack(og_pk, group * 4 + i, 4, og, (group * 4 + i) * 64)
        left = og[pl.ds(pl.multiple_of(group * 256, 256), 256), :]
        for j in range(0, WIDE + 1, 2):
            if j + 1 < WIDE:
                right = w[j * 128:(j + 2) * 128, :]
            else:
                right = jnp.concatenate([w[j * 128:(j + 1) * 128, :], wtail[...]], axis=0)
            out = lax.dot_general(left, right, (((1,), (1,)), ((), ())), preferred_element_type=F32)
            for q in range(8):
                rows = out[q * 32:(q + 1) * 32]
                part[group * 8 + q, j * 4:(j + 1) * 4] = rows[:, :128].reshape(4, 8, 128)
                if j + 1 < WIDE:
                    part[group * 8 + q, (j + 1) * 4:(j + 2) * 4] = rows[:, 128:].reshape(4, 8, 128)
                else:
                    tail = rows[:, 128:].reshape(4, 8, 128)
                    packed = tail[0]
                    for i in range(1, 4):
                        packed = jnp.where(lane == i, tail[i], packed)
                    part[group * 8 + q, 4 * WIDE] = packed

    def cross(zz):
        return remote(part.at[owner_at((xl + 1) % 2, zz), pl.ds(0, SUM_X)], xpart.at[zz],
                      x_send.at[zz], x_recv.at[zz], dl=1)

    def group_of(dy):
        for dx in (0, 1):
            for p in (0, 1):
                shared(dx, dy, p)
        product(dy)

    group_of(0)
    act_step(0, 2)
    act_step(1, 2)
    for p in (0, 1):
        arrived(0, 2, p)
        go(to_core(0, 2, p))
    for dy in (1, 3):
        for p in (0, 1):
            arrived(1, dy, p)
            go(to_core(1, dy, p))
    group_of(1)
    group_of(3)
    for p in (0, 1):
        arrived(1, 2, p)
        go(to_core(1, 2, p))
    act_step(0, 3)
    act_step(1, 3)
    group_of(2)
    for d in range(HALF, 0, -1):
        if "noX" in FLAGS: continue
        go(cross((z + d) % Z))
        if d < HALF:
            go(cross((z + Z - d) % Z))
    if "noX" not in FLAGS: go(cross(z))

    def mine_of(p, zz):
        _, start, size, line = PIECES[p]
        return part.at[owner_at((xl + line) % 2, zz), pl.ds(start, size)]

    def owner_on(way, k):
        d = HALF - k
        return (z + d) % Z if way == 0 else (z + Z - d) % Z

    def sum_hop(way, k, p):
        place, _, size, _ = PIECES[p]
        cut = pl.ds(place, size)
        src = mine_of(p, owner_on(way, k)) if k == FIRST[p][way] else ring.at[way, k - 1, cut]
        return remote(src, ring.at[way, k, cut], s_send.at[way, k, p], s_recv.at[way, k, p],
                      dz=1 if way == 0 else Z - 1)

    def sum_step(k):
        for p in range(4):
            place, start, size, line = PIECES[p]
            for way in (0, 1):
                if k < FIRST[p][way]:
                    continue
                zz = owner_on(way, k)
                mine = mine_of(p, zz)
                if p == 2:
                    cross(zz).wait_recv()
                if k > FIRST[p][way]:
                    sum_hop(way, k - 1, p).wait_recv()
                    cut = pl.ds(place, size)
                    acc = ring[way, k - 1, cut] + mine[...]
                    if p >= 2:
                        acc += xpart[zz, start:start + size]
                    ring[way, k - 1, cut] = acc
                elif p >= 2:
                    mine[...] += xpart[zz, start:start + size]
                go(sum_hop(way, k, p))

    def weight_grad(start, width):
        cols = pl.ds(start, width)
        dw[:, cols] = lax.dot_general(
            act[...], og[:, cols], (((0,), (0,)), ((), ())),
            preferred_element_type=F32).astype(BF16)
        pltpu.make_async_copy(dw.at[:, cols], dw_hbm.at[:, cols], out_sem.at[start // 256]).start()

    for k in range(HALF):
        if "noS" not in FLAGS:
            sum_step(k)
        if k + 4 <= HALF + 1:
            act_step(0, k + 4)
            act_step(1, k + 4)
        if "noDW" in FLAGS:
            continue
        if k == 6:
            for zz in range(Z):
                other = act_pk.at[owner_at((xl + 1) % 2, zz), pl.ds(ACT_X, ACT - ACT_X)]
                remote(other, other, b_send.at[zz], b_recv.at[zz], dl=1).wait_recv()

            @pl.loop(0, 2 * Z)
            def _(place):
                unpack(act_pk, place, 2, act, place * 32)

            weight_grad(0, 256)
            weight_grad(256, 256)
        if k == 7:
            weight_grad(512, 256)
            weight_grad(768, 160)

    def total(p):
        place, start, size, line = PIECES[p]
        acc = mine_of(p, z)[...]
        if p == 2:
            cross(z).wait_recv()
        if p >= 2:
            acc += xpart[z, start:start + size]
        for way in (0, 1):
            if "noS" in FLAGS:
                continue
            sum_hop(way, HALF - 1, p).wait_recv()
            acc += ring[way, HALF - 1, pl.ds(place, size)]
        return acc

    other = mine_of(0, z)
    other[...] = total(0)
    swap = remote(other, last, l_send, l_recv, dl=1)
    go(swap)

    def tiles_out(acc, start):
        for t in range(acc.shape[0]):
            j, i = (start + t) // 4, (start + t) % 4
            if j < WIDE:
                din_ref[8 * i:8 * (i + 1), j * 128:(j + 1) * 128] = acc[t].astype(BF16)
            else:
                for i in range(4):
                    din_ref[8 * i:8 * (i + 1), MAIN:] = acc[t][:, 32 * i:32 * (i + 1)].astype(BF16)

    acc = total(1)
    tiles_out(total(2), 0)
    tiles_out(total(3), SUM_X // 2)
    swap.wait_recv()
    tiles_out(acc + last[...], SUM_X)
    if "noDW" not in FLAGS:
        for i, width in enumerate((256, 256, 256, 160)):
            cols = pl.ds(256 * i, width)
            pltpu.make_async_copy(dw.at[:, cols], dw_hbm.at[:, cols], out_sem.at[i]).wait()
    else:
        for zz in range(Z):
            other = act_pk.at[owner_at((xl + 1) % 2, zz), pl.ds(ACT_X, ACT - ACT_X)]
            if "noC" not in FLAGS: remote(other, other, b_send.at[zz], b_recv.at[zz], dl=1).wait_recv()
    for copy in waits:
        copy.wait_send()


def on_device(activations, out_grad, weight):
    model, hidden = weight.shape
    dma = pltpu.SemaphoreType.DMA
    return pl.pallas_call(
        kernel,
        out_shape=(jax.ShapeDtypeStruct(activations.shape, BF16), jax.ShapeDtypeStruct(weight.shape, BF16)),
        in_specs=[pl.BlockSpec(memory_space=pl.ANY)] * 3,
        out_specs=(pl.BlockSpec(memory_space=pltpu.VMEM), pl.BlockSpec(memory_space=pl.ANY)),
        scratch_shapes=[
            pltpu.VMEM((2 * Z * 32, model), BF16),
            pltpu.VMEM((2 * Z * 32, hidden), BF16),
            pltpu.VMEM((model, hidden), BF16),
            pltpu.VMEM((128, hidden), BF16),
            pltpu.VMEM((2 * Z, ACT, 16, 128), BF16),
            pltpu.VMEM((4 * Y, OG, 16, 128), BF16),
            pltpu.VMEM((2 * Z, SUM, 8, 128), F32),
            pltpu.VMEM((Z, SUM_X, 8, 128), F32),
            pltpu.VMEM((2, HALF, SLOT, 8, 128), F32),
            pltpu.VMEM((LAST, 8, 128), F32),
            pltpu.VMEM((model, hidden), BF16),
            dma((3,)), dma((4,)),
            dma((2, Y, 2)), dma((2, Y, 2)),
            dma((2, Y, 2)), dma((2, Y, 2)),
            dma(()), dma(()),
            dma((Z,)), dma((Z,)),
            dma((2, 2, HALF + 1)), dma((2, 2, HALF + 1)),
            dma((Z,)), dma((Z,)),
            dma((2, HALF, 4)), dma((2, HALF, 4)),
            dma(()), dma(()),
        ],
        compiler_params=pltpu.CompilerParams(
            collective_id=0, has_side_effects=True, vmem_limit_bytes=60 << 20),
        name="backward",
    )(activations, out_grad, weight)


def solution(mesh):
    return jax.shard_map(
        on_device,
        mesh=mesh,
        in_specs=(P("col", "row"), P("row", "col"), P("row", "col")),
        out_specs=(P("col", "row"), P("row", "col")),
        check_vma=False,
    )
```

```python
import jax
import jax.numpy as jnp
from jax import lax
from jax.experimental import pallas as pl
from jax.experimental.pallas import tpu as pltpu
from jax.sharding import PartitionSpec as P

MESH = pl.DeviceIdType.MESH
F32 = jnp.float32
BF16 = jnp.bfloat16
FLAGS = set()
Y, Z = 4, 16
HALF = Z // 2
WIDE = 7
MAIN = WIDE * 128
OG = 4 * WIDE + 1
ACT = 2 * WIDE + 1
ACT_CUT = (0, 8, ACT)
SUM = 4 * WIDE + 1
OG_CUT = (0, 2 * WIDE, OG)
SUM = 2 * WIDE + 1
SPAN = 200.0
FIRST = ((0, 1), (1, 0))


def encode(total, tail):
    top = jnp.maximum(jnp.max(jnp.abs(total.reshape(-1, 8, 128)), axis=0), jnp.abs(tail))
    scale = jnp.maximum(top * 1.01, 1e-30).astype(BF16)
    inverse = SPAN / scale.astype(F32)

    def code(values):
        power = values * inverse
        number = jnp.exp2(jnp.abs(power) - SPAN / 2)
        return jnp.where(power < 0, -number, number)

    main = code(total.reshape(-1, 8, 128)).reshape(total.shape).astype(BF16)
    return main, jnp.concatenate([code(tail), scale.astype(F32)], axis=0).astype(BF16)


def decode(main, rest):
    rest = rest.astype(F32)
    step = rest[8:] * (1 / SPAN)

    def value(number):
        size = jnp.log(jnp.abs(number)) * 1.4426950408889634 + SPAN / 2
        return jnp.where(number < 0, -size, size) * step

    main = main.astype(F32)
    return value(main.reshape(-1, 8, 128)).reshape(main.shape), value(rest[:8])


def kernel(act_hbm, og_hbm, w_hbm, din_ref, dw_hbm,
           act, og, w, wtail, act_pk, og_pk, part, ring, out, last, dw,
           local_sem, out_sem, r_send, r_recv, d_send, d_recv, b_send, b_recv,
           c_send, c_recv, s_send, s_recv, l_send, l_recv):
    row, col = lax.axis_index("row"), lax.axis_index("col")
    xh, y, core = row // 8, (row // 2) % Y, row % 2
    xl, z = col // Z, col % Z

    def device(dx=0, dy=0, dcore=0, dl=0, dz=0):
        r = ((xh + dx) % 2) * 8 + ((y + dy) % Y) * 2 + (core + dcore) % 2
        c = ((xl + dl) % 2) * Z + (z + dz) % Z
        return (r, c)

    def owner_at(line, zz):
        return (zz // 4) * 8 + line * 4 + zz % 4

    def source_at(hi, yy, cc):
        return yy * 4 + hi * 2 + cc

    def remote(src, dst, send, recv, **where):
        return pltpu.make_async_remote_copy(
            src_ref=src, dst_ref=dst, send_sem=send, recv_sem=recv,
            device_id=device(**where), device_id_type=MESH)

    waits = []

    def go(copy):
        copy.start()
        waits.append(copy)

    mine_og, mine_act = source_at(xh, y, core), owner_at(xl, z)
    get_og = pltpu.make_async_copy(
        og_hbm, og.at[pl.ds(pl.multiple_of(mine_og * 64, 64), 64)], local_sem.at[0])
    get_act = pltpu.make_async_copy(
        act_hbm, act.at[pl.ds(pl.multiple_of(mine_act * 32, 32), 32)], local_sem.at[1])
    get_w = pltpu.make_async_copy(w_hbm, w, local_sem.at[2])
    get_og.start()
    get_act.start()
    get_w.start()

    barrier = pltpu.get_barrier_semaphore()
    near = [dict(dx=1), dict(dy=1), dict(dy=3), dict(dy=2),
            dict(dcore=1), dict(dl=1), dict(dz=1), dict(dz=Z - 1),
            dict(dl=1, dz=1), dict(dl=1, dz=Z - 1)]
    for where in near:
        pl.semaphore_signal(barrier, inc=1, device_id=device(**where), device_id_type=MESH)

    def pack(rows_ref, base, groups, pk, place):
        tails = []
        for i in range(groups):
            rows = pl.ds(pl.multiple_of(base + 16 * i, 16), 16)
            for j in range(WIDE):
                pk[place, i * WIDE + j] = rows_ref[rows, j * 128:(j + 1) * 128]
            tails.append(rows_ref[rows, MAIN:])
        pk[place, groups * WIDE, :, :32 * groups] = jnp.concatenate(tails, axis=1)

    def unpack(pk, place, groups, rows_ref, base):
        tails = pk[place, groups * WIDE]
        for i in range(groups):
            rows = pl.ds(pl.multiple_of(base + 16 * i, 16), 16)
            for j in range(WIDE):
                rows_ref[rows, j * 128:(j + 1) * 128] = pk[place, i * WIDE + j]
            rows_ref[rows, MAIN:] = tails[:, 32 * i:32 * (i + 1)]

    get_og.wait()
    pack(og, mine_og * 64, 4, og_pk, mine_og)
    get_act.wait()
    pack(act, mine_act * 32, 2, act_pk, mine_act)
    pl.semaphore_wait(barrier, len(near))

    def og_piece(dx, dy, dcore, p):
        place = source_at((xh + dx) % 2, (y + dy) % Y, (core + dcore) % 2)
        return og_pk.at[place, pl.ds(OG_CUT[p], OG_CUT[p + 1] - OG_CUT[p])]

    def to_x(p):
        ref = og_piece(0, 0, 0, p)
        return remote(ref, ref, r_send.at[1, 0, p], r_recv.at[1, 0, p], dx=1)

    def to_y(dx, dy, p):
        ref = og_piece(dx, 0, 0, p)
        return remote(ref, ref, r_send.at[dx, dy, p], r_recv.at[dx, (Y - dy) % Y, p], dy=dy)

    def over_x(p):
        ref = og_piece(0, 2, 0, p)
        return remote(ref, ref, r_send.at[1, 2, p], r_recv.at[1, 2, p], dx=1)

    def to_core(dx, dy, p):
        ref = og_piece(dx, dy, 0, p)
        return remote(ref, ref, d_send.at[dx, dy, p], d_recv.at[dx, dy, p], dcore=1)

    def arrived(dx, dy, p):
        ref = og_piece(dx, dy, 0, p)
        remote(ref, ref, r_send.at[dx, dy, p], r_recv.at[dx, dy, p], dx=1).wait_recv()

    def shared(dx, dy, p):
        ref = og_piece(dx, dy, 1, p)
        remote(ref, ref, d_send.at[dx, dy, p], d_recv.at[dx, dy, p], dcore=1).wait_recv()

    for p in (0, 1):
        go(to_x(p))
    for p in (0, 1):
        for dy in (1, 3):
            go(to_y(0, dy, p))
    for p in (0, 1):
        go(to_y(0, 2, p))

    def act_piece(line, zz, p):
        return act_pk.at[owner_at((xl + line) % 2, zz), pl.ds(ACT_CUT[p], ACT_CUT[p + 1] - ACT_CUT[p])]

    def act_x(line, zz, p):
        ref = act_piece(line, zz, p)
        return remote(ref, ref, b_send.at[zz, p], b_recv.at[zz, p], dl=1)

    def back(way, step):
        return (z - step) % Z if way == 0 else (z + step) % Z

    def act_hop(way, step, p):
        ref = act_piece(0, back(way, step - 1), p)
        return remote(ref, ref, c_send.at[way, step, p], c_recv.at[way, step, p], dz=1 if way == 0 else Z - 1)

    hops = (HALF, HALF - 1)

    def act_step(step):
        if "noC" in FLAGS:
            return
        for p in (0, 1):
            for way in (0, 1):
                if 2 <= step <= hops[way] + 1:
                    act_hop(way, step - 1, p).wait_recv()
                if step <= hops[way]:
                    go(act_hop(way, step, p))
        for p in (0, 1):
            for way in (0, 1):
                if 2 <= step <= hops[way] + 1:
                    go(act_x(0, back(way, step - 1), p))

    act_step(1)
    if "noC" not in FLAGS:
        for p in (0, 1):
            go(act_x(0, z, p))
    for p in (0, 1):
        go(to_core(0, 0, p))

    get_w.wait()
    for i in range(4):
        wtail[32 * i:32 * (i + 1), :] = w[MAIN:, :]

    for p in (0, 1):
        arrived(1, 0, p)
        for dy in (1, 3):
            go(to_y(1, dy, p))
        if p == 0:
            go(to_y(1, 2, p))
        go(to_core(1, 0, p))
    for p in (0, 1):
        for dy in (1, 3):
            arrived(0, dy, p)
            go(to_core(0, dy, p))
    for p in (1, 0):
        arrived(0, 2, p)
        if p == 1:
            go(over_x(p))
        go(to_core(0, 2, p))
    act_step(2)

    lane = lax.broadcasted_iota(jnp.int32, (8, 128), 1) // 32

    def product(dy):
        group = (y + dy) % Y
        if "noP" in FLAGS:
            return
        for i in range(4):
            unpack(og_pk, group * 4 + i, 4, og, (group * 4 + i) * 64)
        left = og[pl.ds(pl.multiple_of(group * 256, 256), 256), :]
        for j in range(0, WIDE + 1, 2):
            if j + 1 < WIDE:
                right = w[j * 128:(j + 2) * 128, :]
            else:
                right = jnp.concatenate([w[j * 128:(j + 1) * 128, :], wtail[...]], axis=0)
            out = lax.dot_general(left, right, (((1,), (1,)), ((), ())), preferred_element_type=F32)
            for q in range(8):
                rows = out[q * 32:(q + 1) * 32]
                part[group * 8 + q, j * 2:(j + 1) * 2] = rows[:, :128].reshape(2, 16, 128)
                if j + 1 < WIDE:
                    part[group * 8 + q, (j + 1) * 2:(j + 2) * 2] = rows[:, 128:].reshape(2, 16, 128)
                else:
                    tail = rows[:, 128:].reshape(4, 8, 128)
                    packed = tail[0]
                    for i in range(1, 4):
                        packed = jnp.where(lane == i, tail[i], packed)
                    part[group * 8 + q, 2 * WIDE, :8] = packed

    def group_of(dy):
        for dx in (0, 1):
            for p in (0, 1):
                shared(dx, dy, p)
        product(dy)

    group_of(0)
    for p in (0, 1):
        for dy in (1, 3):
            arrived(1, dy, p)
            go(to_core(1, dy, p))
    group_of(1)
    act_step(3)
    for p in (0, 1):
        arrived(1, 2, p)
        go(to_core(1, 2, p))
    group_of(3)
    group_of(2)

    def owner_on(way, k):
        return (z + HALF - k) % Z if way == 0 else (z + HALF + k) % Z

    def mine_of(line, zz):
        place = owner_at((xl + line) % 2, zz)
        return part[place, :2 * WIDE], part[place, 2 * WIDE, :8]

    def sum_hop(way, k, line):
        return remote(out.at[way, k, line], ring.at[way, k, line], s_send.at[way, k, line], s_recv.at[way, k, line],
                      dl=1 if k == HALF - 1 and line == 1 else 0, dz=1 if way == 0 else Z - 1)

    def arrived_sum(way, k, line):
        sum_hop(way, k, line).wait_recv()
        return decode(ring[way, k, line, :2 * WIDE], ring[way, k, line, 2 * WIDE])

    def put(ref, main, rest):
        ref[:2 * WIDE] = main
        ref[2 * WIDE] = rest

    def sum_step(k):
        for line in (1, 0):
            for way in (0, 1):
                if k < FIRST[line][way]:
                    continue
                main, tail = mine_of(line, owner_on(way, k))
                if k > FIRST[line][way]:
                    more, rest = arrived_sum(way, k - 1, line)
                    main, tail = main + more, tail + rest
                put(out.at[way, k, line], *encode(main, tail))
                go(sum_hop(way, k, line))

    def weight_grad(start, width):
        cols = pl.ds(start, width)
        dw[:, cols] = lax.dot_general(
            act[...], og[:, cols], (((0,), (0,)), ((), ())),
            preferred_element_type=F32).astype(BF16)
        pltpu.make_async_copy(dw.at[:, cols], dw_hbm.at[:, cols], out_sem.at[start // 256]).start()

    swap = remote(last.at[0], last.at[1], l_send, l_recv, dl=1)
    for k in range(HALF):
        if "noS" not in FLAGS:
            sum_step(k)
        if k == 0:
            put(last.at[0], *encode(*mine_of(1, z)))
            go(swap)
        if k + 4 <= HALF + 1:
            act_step(k + 4)
        if "noDW" in FLAGS:
            continue
        if k == 6:
            for zz in range(Z):
                for p in (0, 1):
                    act_x(1, zz, p).wait_recv()

            @pl.loop(0, 2 * Z)
            def _(place):
                unpack(act_pk, place, 2, act, place * 32)

            weight_grad(0, 256)
        if k == 7:
            weight_grad(256, 256)
            weight_grad(512, 256)
            weight_grad(768, 160)

    main, tail = mine_of(0, z)
    swap.wait_recv()
    for more, rest in [decode(last[1, :2 * WIDE], last[1, 2 * WIDE])] + [
            arrived_sum(way, HALF - 1, line) for line in (0, 1) for way in (0, 1) if "noS" not in FLAGS]:
        main, tail = main + more, tail + rest
    for j in range(WIDE):
        din_ref[:, j * 128:(j + 1) * 128] = main[2 * j:2 * j + 2].reshape(32, 128).astype(BF16)
    for i in range(0, 4, 2):
        pair = [tail[:, 32 * (i + h):32 * (i + h + 1)] for h in (0, 1)]
        din_ref[8 * i:8 * i + 16, MAIN:] = jnp.concatenate(pair, axis=0).astype(BF16)
    if "noDW" not in FLAGS:
        for i, width in enumerate((256, 256, 256, 160)):
            cols = pl.ds(256 * i, width)
            pltpu.make_async_copy(dw.at[:, cols], dw_hbm.at[:, cols], out_sem.at[i]).wait()
    if "noDW" in FLAGS and "noC" not in FLAGS:
        for zz in range(Z):
            for p in (0, 1):
                act_x(1, zz, p).wait_recv()
    for copy in waits:
        copy.wait_send()


def hand_over(din_in, dw_in, din_out, dw_out):
    din_out[...] = din_in[...]
    dw_out[...] = dw_in[...]


def on_device(activations, out_grad, weight):
    model, hidden = weight.shape
    dma = pltpu.SemaphoreType.DMA
    din, dw = pl.pallas_call(
        kernel,
        out_shape=(jax.ShapeDtypeStruct(activations.shape, BF16), jax.ShapeDtypeStruct(weight.shape, BF16)),
        in_specs=[pl.BlockSpec(memory_space=pl.ANY)] * 3,
        out_specs=(pl.BlockSpec(memory_space=pltpu.VMEM), pl.BlockSpec(memory_space=pl.ANY)),
        scratch_shapes=[
            pltpu.VMEM((2 * Z * 32, model), BF16),
            pltpu.VMEM((2 * Z * 32, hidden), BF16),
            pltpu.VMEM((model, hidden), BF16),
            pltpu.VMEM((128, hidden), BF16),
            pltpu.VMEM((2 * Z, ACT, 16, 128), BF16),
            pltpu.VMEM((4 * Y, OG, 16, 128), BF16),
            pltpu.VMEM((2 * Z, SUM, 16, 128), F32),
            pltpu.VMEM((2, HALF, 2, SUM, 16, 128), BF16),
            pltpu.VMEM((2, HALF, 2, SUM, 16, 128), BF16),
            pltpu.VMEM((2, SUM, 16, 128), BF16),
            pltpu.VMEM((model, hidden), BF16),
            dma((3,)), dma((4,)),
            dma((2, Y, 2)), dma((2, Y, 2)),
            dma((2, Y, 2)), dma((2, Y, 2)),
            dma((Z, 2)), dma((Z, 2)),
            dma((2, HALF + 1, 2)), dma((2, HALF + 1, 2)),
            dma((2, HALF, 2)), dma((2, HALF, 2)),
            dma(()), dma(()),
        ],
        compiler_params=pltpu.CompilerParams(
            collective_id=0, has_side_effects=True, vmem_limit_bytes=60 << 20),
        name="backward",
    )(activations, out_grad, weight)
    return pl.pallas_call(
        hand_over,
        out_shape=(jax.ShapeDtypeStruct(din.shape, BF16), jax.ShapeDtypeStruct(dw.shape, BF16)),
        grid=(2,),
        in_specs=[pl.BlockSpec((16, model), lambda i: (i, 0)), pl.BlockSpec((model // 2, hidden), lambda i: (i, 0))],
        out_specs=[pl.BlockSpec((16, model), lambda i: (i, 0)), pl.BlockSpec((model // 2, hidden), lambda i: (i, 0))],
        name="outputs",
    )(din, dw)


def solution(mesh):
    return jax.shard_map(
        on_device,
        mesh=mesh,
        in_specs=(P("col", "row"), P("row", "col"), P("row", "col")),
        out_specs=(P("col", "row"), P("row", "col")),
        check_vma=False,
    )
```

```python
import jax
import jax.numpy as jnp
from jax import lax
from jax.experimental import pallas as pl
from jax.experimental.pallas import tpu as pltpu
from jax.sharding import PartitionSpec as P

MESH = pl.DeviceIdType.MESH
F32 = jnp.float32
BF16 = jnp.bfloat16
Y, Z = 4, 16
HALF = Z // 2
WIDE = 7
MAIN = WIDE * 128
OG = 4 * WIDE + 1
ACT = 2 * WIDE + 1
ACT_CUT = (0, 8, ACT)
SUM = 4 * WIDE + 1
OG_CUT = (0, 2 * WIDE, OG)
SUM = 2 * WIDE + 1
SPAN = 200.0
FIRST = ((0, 1), (1, 0))


def encode(total, tail):
    top = jnp.maximum(jnp.max(jnp.abs(total.reshape(-1, 8, 128)), axis=0), jnp.abs(tail))
    scale = jnp.maximum(top * 1.01, 1e-30).astype(BF16)
    inverse = SPAN / scale.astype(F32)

    def code(values):
        power = values * inverse
        number = jnp.exp2(jnp.abs(power) - SPAN / 2)
        return jnp.where(power < 0, -number, number)

    main = code(total.reshape(-1, 8, 128)).reshape(total.shape).astype(BF16)
    return main, jnp.concatenate([code(tail), scale.astype(F32)], axis=0).astype(BF16)


def decode(main, rest):
    rest = rest.astype(F32)
    step = rest[8:] * (1 / SPAN)

    def value(number):
        size = jnp.log(jnp.abs(number)) * 1.4426950408889634 + SPAN / 2
        return jnp.where(number < 0, -size, size) * step

    main = main.astype(F32)
    return value(main.reshape(-1, 8, 128)).reshape(main.shape), value(rest[:8])


def kernel(act_hbm, og_hbm, w_hbm, din_ref, dw_hbm,
           act, og, w, wtail, act_pk, og_pk, part, ring, out, last, dw,
           local_sem, out_sem, r_send, r_recv, d_send, d_recv, b_send, b_recv,
           c_send, c_recv, s_send, s_recv, l_send, l_recv):
    row, col = lax.axis_index("row"), lax.axis_index("col")
    xh, y, core = row // 8, (row // 2) % Y, row % 2
    xl, z = col // Z, col % Z

    def device(dx=0, dy=0, dcore=0, dl=0, dz=0):
        r = ((xh + dx) % 2) * 8 + ((y + dy) % Y) * 2 + (core + dcore) % 2
        c = ((xl + dl) % 2) * Z + (z + dz) % Z
        return (r, c)

    def owner_at(line, zz):
        return (zz // 4) * 8 + line * 4 + zz % 4

    def source_at(hi, yy, cc):
        return yy * 4 + hi * 2 + cc

    def remote(src, dst, send, recv, **where):
        return pltpu.make_async_remote_copy(
            src_ref=src, dst_ref=dst, send_sem=send, recv_sem=recv,
            device_id=device(**where), device_id_type=MESH)

    waits = []

    def go(copy):
        copy.start()
        waits.append(copy)

    mine_og, mine_act = source_at(xh, y, core), owner_at(xl, z)
    get_og = pltpu.make_async_copy(
        og_hbm, og.at[pl.ds(pl.multiple_of(mine_og * 64, 64), 64)], local_sem.at[0])
    get_act = pltpu.make_async_copy(
        act_hbm, act.at[pl.ds(pl.multiple_of(mine_act * 32, 32), 32)], local_sem.at[1])
    get_w = pltpu.make_async_copy(w_hbm, w, local_sem.at[2])
    get_og.start()
    get_act.start()
    get_w.start()

    barrier = pltpu.get_barrier_semaphore()
    near = [dict(dx=1), dict(dy=1), dict(dy=3), dict(dy=2),
            dict(dcore=1), dict(dl=1), dict(dz=1), dict(dz=Z - 1),
            dict(dl=1, dz=1), dict(dl=1, dz=Z - 1)]
    for where in near:
        pl.semaphore_signal(barrier, inc=1, device_id=device(**where), device_id_type=MESH)

    def pack(rows_ref, base, groups, pk, place):
        tails = []
        for i in range(groups):
            rows = pl.ds(pl.multiple_of(base + 16 * i, 16), 16)
            for j in range(WIDE):
                pk[place, i * WIDE + j] = rows_ref[rows, j * 128:(j + 1) * 128]
            tails.append(rows_ref[rows, MAIN:])
        pk[place, groups * WIDE, :, :32 * groups] = jnp.concatenate(tails, axis=1)

    def unpack(pk, place, groups, rows_ref, base):
        tails = pk[place, groups * WIDE]
        for i in range(groups):
            rows = pl.ds(pl.multiple_of(base + 16 * i, 16), 16)
            for j in range(WIDE):
                rows_ref[rows, j * 128:(j + 1) * 128] = pk[place, i * WIDE + j]
            rows_ref[rows, MAIN:] = tails[:, 32 * i:32 * (i + 1)]

    get_og.wait()
    pack(og, mine_og * 64, 4, og_pk, mine_og)
    pl.semaphore_wait(barrier, len(near))

    def og_piece(dx, dy, dcore, p):
        place = source_at((xh + dx) % 2, (y + dy) % Y, (core + dcore) % 2)
        return og_pk.at[place, pl.ds(OG_CUT[p], OG_CUT[p + 1] - OG_CUT[p])]

    def to_x(p):
        ref = og_piece(0, 0, 0, p)
        return remote(ref, ref, r_send.at[1, 0, p], r_recv.at[1, 0, p], dx=1)

    def to_y(dx, dy, p):
        ref = og_piece(dx, 0, 0, p)
        return remote(ref, ref, r_send.at[dx, dy, p], r_recv.at[dx, (Y - dy) % Y, p], dy=dy)

    def over_x(dy):
        ref = og_piece(0, dy, 0, 1)
        return remote(ref, ref, r_send.at[1, dy, 1], r_recv.at[1, dy, 1], dx=1)

    def to_core(dx, dy, p):
        ref = og_piece(dx, dy, 0, p)
        return remote(ref, ref, d_send.at[dx, dy, p], d_recv.at[dx, dy, p], dcore=1)

    def arrived(dx, dy, p):
        ref = og_piece(dx, dy, 0, p)
        remote(ref, ref, r_send.at[dx, dy, p], r_recv.at[dx, dy, p], dx=1).wait_recv()

    def shared(dx, dy, p):
        ref = og_piece(dx, dy, 1, p)
        remote(ref, ref, d_send.at[dx, dy, p], d_recv.at[dx, dy, p], dcore=1).wait_recv()

    for p in (0, 1):
        go(to_x(p))
    go(to_y(0, 2, 1))
    for p in (1, 0):
        for dy in (1, 3):
            go(to_y(0, dy, p))
    go(to_y(0, 2, 0))

    def act_piece(line, zz, p):
        return act_pk.at[owner_at((xl + line) % 2, zz), pl.ds(ACT_CUT[p], ACT_CUT[p + 1] - ACT_CUT[p])]

    def act_x(line, zz, p):
        ref = act_piece(line, zz, p)
        return remote(ref, ref, b_send.at[zz, p], b_recv.at[zz, p], dl=1)

    def back(way, step):
        return (z - step) % Z if way == 0 else (z + step) % Z

    def act_hop(way, step, p):
        ref = act_piece(0, back(way, step - 1), p)
        return remote(ref, ref, c_send.at[way, step, p], c_recv.at[way, step, p], dz=1 if way == 0 else Z - 1)

    hops = (HALF, HALF - 1)

    def act_step(step):
        for p in (0, 1):
            for way in (0, 1):
                if 2 <= step <= hops[way] + 1:
                    act_hop(way, step - 1, p).wait_recv()
                if step <= hops[way]:
                    go(act_hop(way, step, p))
        for p in (0, 1):
            for way in (0, 1):
                if 2 <= step <= hops[way] + 1:
                    go(act_x(0, back(way, step - 1), p))

    get_act.wait()
    pack(act, mine_act * 32, 2, act_pk, mine_act)
    act_step(1)
    for p in (0, 1):
        go(act_x(0, z, p))
    for p in (0, 1):
        go(to_core(0, 0, p))

    get_w.wait()
    for i in range(4):
        wtail[32 * i:32 * (i + 1), :] = w[MAIN:, :]

    arrived(1, 0, 0)
    for dy in (1, 3, 2):
        go(to_y(1, dy, 0))
    for dy in (2, 1, 3):
        arrived(0, dy, 1)
        go(over_x(dy))
    arrived(1, 0, 1)
    for p in (0, 1):
        go(to_core(1, 0, p))
    for dy in (1, 3, 2):
        arrived(0, dy, 0)
        for p in (1, 0):
            go(to_core(0, dy, p))
    act_step(2)

    lane = lax.broadcasted_iota(jnp.int32, (8, 128), 1) // 32

    def product(dy):
        group = (y + dy) % Y
        for i in range(4):
            unpack(og_pk, group * 4 + i, 4, og, (group * 4 + i) * 64)
        left = og[pl.ds(pl.multiple_of(group * 256, 256), 256), :]
        for j in range(0, WIDE + 1, 2):
            if j + 1 < WIDE:
                right = w[j * 128:(j + 2) * 128, :]
            else:
                right = jnp.concatenate([w[j * 128:(j + 1) * 128, :], wtail[...]], axis=0)
            out = lax.dot_general(left, right, (((1,), (1,)), ((), ())), preferred_element_type=F32)
            for q in range(8):
                rows = out[q * 32:(q + 1) * 32]
                part[group * 8 + q, j * 2:(j + 1) * 2] = rows[:, :128].reshape(2, 16, 128)
                if j + 1 < WIDE:
                    part[group * 8 + q, (j + 1) * 2:(j + 2) * 2] = rows[:, 128:].reshape(2, 16, 128)
                else:
                    tail = rows[:, 128:].reshape(4, 8, 128)
                    packed = tail[0]
                    for i in range(1, 4):
                        packed = jnp.where(lane == i, tail[i], packed)
                    part[group * 8 + q, 2 * WIDE, :8] = packed

    def group_of(dy):
        for dx in (0, 1):
            for p in (0, 1):
                shared(dx, dy, p)
        product(dy)

    group_of(0)
    for p in (0, 1):
        for dy in (1, 3):
            arrived(1, dy, p)
            go(to_core(1, dy, p))
    group_of(1)
    act_step(3)
    for p in (0, 1):
        arrived(1, 2, p)
        go(to_core(1, 2, p))
    group_of(3)
    group_of(2)

    def owner_on(way, k):
        return (z + HALF - k) % Z if way == 0 else (z + HALF + k) % Z

    def mine_of(line, zz):
        place = owner_at((xl + line) % 2, zz)
        return part[place, :2 * WIDE], part[place, 2 * WIDE, :8]

    def sum_hop(way, k, line):
        return remote(out.at[way, k, line], ring.at[way, k, line], s_send.at[way, k, line], s_recv.at[way, k, line],
                      dl=1 if k == HALF - 1 and line == 1 else 0, dz=1 if way == 0 else Z - 1)

    def arrived_sum(way, k, line):
        sum_hop(way, k, line).wait_recv()
        return decode(ring[way, k, line, :2 * WIDE], ring[way, k, line, 2 * WIDE])

    def put(ref, main, rest):
        ref[:2 * WIDE] = main
        ref[2 * WIDE] = rest

    def sum_send(way, k, line, main, tail):
        put(out.at[way, k, line], *encode(main, tail))
        go(sum_hop(way, k, line))

    def sum_step(k):
        if k == 0:
            for first in (0, 1):
                for line in (1, 0):
                    for way in (0, 1):
                        if FIRST[line][way] == first:
                            sum_send(way, first, line, *mine_of(line, owner_on(way, first)))
            return
        for line in (1, 0):
            for way in (0, 1):
                if k <= FIRST[line][way]:
                    continue
                main, tail = mine_of(line, owner_on(way, k))
                more, rest = arrived_sum(way, k - 1, line)
                sum_send(way, k, line, main + more, tail + rest)

    def weight_grad(start, width):
        cols = pl.ds(start, width)
        dw[:, cols] = lax.dot_general(
            act[...], og[:, cols], (((0,), (0,)), ((), ())),
            preferred_element_type=F32).astype(BF16)
        pltpu.make_async_copy(dw.at[:, cols], dw_hbm.at[:, cols], out_sem.at[start // 256]).start()

    swap = remote(last.at[0], last.at[1], l_send, l_recv, dl=1)
    for k in range(HALF):
        sum_step(k)
        if k == 0:
            put(last.at[0], *encode(*mine_of(1, z)))
            go(swap)
        if k + 4 <= HALF + 1:
            act_step(k + 4)
        if k == 6:
            for zz in range(Z):
                for p in (0, 1):
                    act_x(1, zz, p).wait_recv()

            @pl.loop(0, 2 * Z)
            def _(place):
                unpack(act_pk, place, 2, act, place * 32)

            weight_grad(0, 256)
        if k == 7:
            weight_grad(256, 256)
            weight_grad(512, 256)
            weight_grad(768, 160)

    main, tail = mine_of(0, z)
    swap.wait_recv()
    for more, rest in [decode(last[1, :2 * WIDE], last[1, 2 * WIDE])] + [
            arrived_sum(way, HALF - 1, line) for line in (0, 1) for way in (0, 1)]:
        main, tail = main + more, tail + rest
    for j in range(WIDE):
        din_ref[:, j * 128:(j + 1) * 128] = main[2 * j:2 * j + 2].reshape(32, 128).astype(BF16)
    for i in range(0, 4, 2):
        pair = [tail[:, 32 * (i + h):32 * (i + h + 1)] for h in (0, 1)]
        din_ref[8 * i:8 * i + 16, MAIN:] = jnp.concatenate(pair, axis=0).astype(BF16)
    for i, width in enumerate((256, 256, 256, 160)):
        cols = pl.ds(256 * i, width)
        pltpu.make_async_copy(dw.at[:, cols], dw_hbm.at[:, cols], out_sem.at[i]).wait()
    for copy in waits:
        copy.wait_send()


def hand_over(din_in, dw_in, din_out, dw_out, din, dw, sem_in, sem_out):
    rows = [pl.ds(i, min(256, dw_in.shape[0] - i)) for i in range(0, dw_in.shape[0], 256)]
    parts = [(dw_in.at[r], dw.at[r], dw_out.at[r]) for r in rows] + [(din_in, din, din_out)]
    ins = [pltpu.make_async_copy(a, b, sem_in.at[i]) for i, (a, b, _) in enumerate(parts)]
    outs = [pltpu.make_async_copy(b, c, sem_out.at[i]) for i, (_, b, c) in enumerate(parts)]
    for copy in ins:
        copy.start()
    for got, put in zip(ins, outs):
        got.wait()
        put.start()
    for put in outs:
        put.wait()


def on_device(activations, out_grad, weight):
    model, hidden = weight.shape
    dma = pltpu.SemaphoreType.DMA
    din, dw = pl.pallas_call(
        kernel,
        out_shape=(jax.ShapeDtypeStruct(activations.shape, BF16), jax.ShapeDtypeStruct(weight.shape, BF16)),
        in_specs=[pl.BlockSpec(memory_space=pl.ANY)] * 3,
        out_specs=(pl.BlockSpec(memory_space=pltpu.VMEM), pl.BlockSpec(memory_space=pl.ANY)),
        scratch_shapes=[
            pltpu.VMEM((2 * Z * 32, model), BF16),
            pltpu.VMEM((2 * Z * 32, hidden), BF16),
            pltpu.VMEM((model, hidden), BF16),
            pltpu.VMEM((128, hidden), BF16),
            pltpu.VMEM((2 * Z, ACT, 16, 128), BF16),
            pltpu.VMEM((4 * Y, OG, 16, 128), BF16),
            pltpu.VMEM((2 * Z, SUM, 16, 128), F32),
            pltpu.VMEM((2, HALF, 2, SUM, 16, 128), BF16),
            pltpu.VMEM((2, HALF, 2, SUM, 16, 128), BF16),
            pltpu.VMEM((2, SUM, 16, 128), BF16),
            pltpu.VMEM((model, hidden), BF16),
            dma((3,)), dma((4,)),
            dma((2, Y, 2)), dma((2, Y, 2)),
            dma((2, Y, 2)), dma((2, Y, 2)),
            dma((Z, 2)), dma((Z, 2)),
            dma((2, HALF + 1, 2)), dma((2, HALF + 1, 2)),
            dma((2, HALF, 2)), dma((2, HALF, 2)),
            dma(()), dma(()),
        ],
        compiler_params=pltpu.CompilerParams(
            collective_id=0, has_side_effects=True, vmem_limit_bytes=60 << 20),
        name="backward",
    )(activations, out_grad, weight)
    return pl.pallas_call(
        hand_over,
        out_shape=(jax.ShapeDtypeStruct(din.shape, BF16), jax.ShapeDtypeStruct(dw.shape, BF16)),
        in_specs=[pl.BlockSpec(memory_space=pl.ANY)] * 2,
        out_specs=[pl.BlockSpec(memory_space=pl.ANY)] * 2,
        scratch_shapes=[pltpu.VMEM(din.shape, BF16), pltpu.VMEM(dw.shape, BF16),
                        pltpu.SemaphoreType.DMA((5,)), pltpu.SemaphoreType.DMA((5,))],
        compiler_params=pltpu.CompilerParams(vmem_limit_bytes=60 << 20),
        name="outputs",
    )(din, dw)


def solution(mesh):
    return jax.shard_map(
        on_device,
        mesh=mesh,
        in_specs=(P("col", "row"), P("row", "col"), P("row", "col")),
        out_specs=(P("col", "row"), P("row", "col")),
        check_vma=False,
    )
```
